32 devices in a mesh: groups: 2 (over x), lon: 16 (over z, y, core).
Axes of the slice: x: 2, y: 2, z: 4, core: 2. Of those that a mesh axis runs over, the one named last changes fastest.
Arguments:
- inputs: bfloat16 [16, 896, 512], P('groups', 'lon'), parts along dimension 0, may hold values from -6 to 6
- support: int32 [16], P('groups'), parts along dimension 0, may hold values from 1 to 4, as said below
- basis_table: bfloat16 [9, 16, 3, 449], P(None, 'groups'), parts along dimension 1, may hold values from -0.15625 to 0.15625
- mixing: bfloat16 [4608, 512], P('lon'), may hold values from -0.09375 to 0.09375
Outputs:
- output_field: bfloat16 [16, 896, 512], P('groups', 'lon'), parts along dimension 0
The draws below stay inside these ranges and needn't reach their ends.
There are 2 independent parts, one for each index of `groups`. The reference program is written for one: setup_inputs(seed, part) draws one part's arguments, and reference() takes and returns one part's arrays. A program takes and returns all parts, laid end to end along the dimension named above; an argument that names none is the same for every part. Nothing has to cross between parts.
Inputs may be any that keep to these rules, and one draw needn't show every extreme that they name: `support`: in the first slab some band reaches 4.
All inputs are finite; a program needn't handle non-finite values.
Results may differ from the reference program's by a relative error of at most 0.0051.
Values may be sent and summed in bfloat16 or wider, within the bound.
No kernel may reach another device: no remote copies, remote signals or barrier semaphores. Data moves between devices by JAX's collectives and lax.ppermute only.
A program may use at most 64 MiB of HBM per device.

```python
import jax
import jax.numpy as jnp

C = 512
K = 9
LAT = 8
LON_DEV = 56
MAXS = 4
OFF = 449
NLON = 896
N_LON = 16


def draw_support(key, part):
    key = jax.random.fold_in(key, 1)
    first_key, second_key = jax.random.split(key)
    widths = jax.random.randint(first_key, (LAT,), 1, MAXS + 1).astype(jnp.int32)
    widest = jax.random.randint(second_key, (), 0, LAT).astype(jnp.int32)
    bands = jnp.arange(LAT).astype(jnp.int32)
    polar = jnp.asarray(part) == 0
    forced = jnp.logical_and(polar, bands == widest)
    return jnp.where(forced, MAXS, widths).astype(jnp.int32)


def levels(rng, dims, cuts, least, largest):
    gain = 1.0
    for dim, shards_of in cuts:
        steps = jax.random.uniform(jax.random.fold_in(jax.random.fold_in(rng, 6), dim), (shards_of,), jnp.float32, least / len(cuts), largest / len(cuts))
        gain = gain * jnp.repeat(jnp.exp(steps), dims[dim] // shards_of).reshape((-1,) + (1,) * (len(dims) - 1 - dim))
    return gain


def noise(stream_key, extent, scale, reach, shards=(), held_as=jnp.bfloat16):
    loudness = levels(stream_key, extent, shards, -0.22, 0.18) if shards else 1.0
    result = jax.random.normal(stream_key, extent, jnp.float32) * scale * loudness
    return jnp.minimum(jnp.maximum(result, -reach), reach).astype(held_as)


def setup_inputs(seed: int = 0, part: int = 0) -> dict:
    key_of = jax.random.split(jax.random.key(seed), 5)
    part_keys = jax.random.split(jax.random.fold_in(key_of[4], part), 5)
    return {
        "inputs": noise(part_keys[0], (LAT, NLON, C), 1.0, 6.0, ((1, 16),)),
        "support": draw_support(jax.random.fold_in(jax.random.fold_in(key_of[4], part), 71), part),
        "basis_table": noise(part_keys[2], (K, LAT, 3, OFF), (3 * OFF) ** -0.5, 0.15625),
        "mixing": noise(key_of[3], (K * C, C), (K * C) ** -0.5, 0.09375, ((0, 16),)),
    }


def blocks_basis(basis_table, support, block_shift):
    out_pos = jnp.arange(LON_DEV)[:, None]
    in_pos = jnp.arange(LON_DEV)[None, :]
    offsets = block_shift * LON_DEV + in_pos - out_pos
    offset_index = jnp.clip(offsets + MAXS * LON_DEV, 0, 2 * MAXS * LON_DEV).astype(jnp.int32)
    picked = jnp.take(basis_table, offset_index, axis=3)
    within = jnp.abs(offsets)[None, :, :] <= (support * LON_DEV)[:, None, None]
    return jnp.where(within[None, :, None, :, :], picked, jnp.zeros_like(picked))


def reference(inputs, support, basis_table, mixing):
    blocked = inputs.astype(jnp.float32).reshape(LAT, N_LON, LON_DEV, C)
    padded = jnp.pad(blocked, ((1, 1), (0, 0), (0, 0), (0, 0)))
    windows = jnp.stack([padded[lat_shift:lat_shift + LAT] for lat_shift in range(3)])
    convolved = jnp.zeros((LAT, N_LON, LON_DEV, K, C), jnp.float32)
    for block_shift in range(-MAXS, MAXS + 1):
        toeplitz = blocks_basis(basis_table, support, block_shift).astype(jnp.float32)
        rolled = jnp.roll(windows, -block_shift, axis=2)
        convolved = convolved + jnp.einsum('kiwab,widbc->idakc', toeplitz, rolled)
    flattened = convolved.astype(jnp.bfloat16).reshape(LAT * N_LON * LON_DEV, K * C)
    summed = jnp.dot(flattened, mixing, preferred_element_type=jnp.float32)
    return jax.nn.gelu(summed).astype(jnp.bfloat16).reshape(LAT, N_LON * LON_DEV, C)
```

```python
import jax
import jax.numpy as jnp
from jax import lax
from jax.experimental import pallas as pl
from jax.experimental.pallas import tpu as pltpu
from jax.sharding import PartitionSpec as P

MAXS = 4
UNIT = 16
VMEM = 48 << 20


def send(value, axis, target_of):
    count = lax.axis_size(axis)
    return lax.ppermute(value, axis, [(s, target_of(s)) for s in range(count)])


def round_up(value, step):
    return -(-value // step) * step


def packed_basis(basis_table, support, longitudes, segment):
    filters, bands, three, offsets = basis_table.shape
    distance = jnp.abs(jnp.arange(offsets) - MAXS * longitudes)
    within = distance[None, :] <= (support * longitudes)[:, None]
    rows = jnp.where(within[None, :, None, :], basis_table, jnp.zeros_like(basis_table))
    rows = jnp.pad(rows, ((0, 0), (0, 0), (0, 0), (0, segment - offsets)))
    rows = rows.transpose(1, 0, 2, 3).reshape(bands, filters, three * segment)
    return rows.astype(jnp.float32)


def toeplitz(packed, longitudes):
    bands, filters, lanes = packed.shape
    rows = round_up(filters * longitudes, UNIT)

    def body(packed_ref, out_ref):
        def block(k):
            row = jnp.broadcast_to(packed_ref[0, k : k + 1, :], (longitudes, lanes))
            return pltpu.roll(row, 0, 1, stride=1, stride_axis=0)

        for k in range(0, filters, 2):
            start = k * longitudes
            if k + 1 < filters:
                pair = jnp.concatenate([block(k), block(k + 1)], 0)
            else:
                tail = jnp.zeros((rows - start - longitudes, lanes), jnp.float32)
                pair = jnp.concatenate([block(k), tail], 0)
            out_ref[0, start : start + pair.shape[0], :] = pair.astype(jnp.bfloat16)

    return pl.pallas_call(
        body,
        grid=(bands,),
        in_specs=[pl.BlockSpec((1, filters, lanes), lambda i: (i, 0, 0))],
        out_specs=pl.BlockSpec((1, rows, lanes), lambda i: (i, 0, 0)),
        out_shape=jax.ShapeDtypeStruct((bands, rows, lanes), jnp.bfloat16),
        compiler_params=pltpu.CompilerParams(vmem_limit_bytes=VMEM),
        name="toeplitz",
    )(packed)


def convolve_and_mix(place, matrices, planes, weights, filters):
    _, bands, longitudes, chans = planes[0].shape
    rows, lanes = matrices.shape[1:]
    segment = lanes // 3
    span = 3 * MAXS * longitudes
    window = (2 * MAXS + 1) * longitudes
    outs = weights.shape[1]
    used = filters * longitudes

    def body(place_ref, t_ref, west_ref, own_ref, east_ref, w_ref, mine_ref, rest_ref, line, windows):
        band = pl.program_id(0)
        here = place_ref[0]

        def fill(b):
            for t, ref in enumerate((west_ref, own_ref, east_ref)):
                for p in range(MAXS):
                    start = (t * MAXS + p) * longitudes
                    line[start : start + longitudes, :] = ref[p ^ here, b].astype(jnp.float32)
            for r in range(MAXS):
                first = pl.multiple_of((r ^ here) * longitudes, 8)
                part = line[pl.ds(first, segment), :].astype(jnp.bfloat16)
                start = pl.multiple_of((b + 1) * segment, segment)
                windows[pl.ds(start, segment), r * chans : (r + 1) * chans] = part

        @pl.when(band == 0)
        def _():
            line[span:, :] = jnp.zeros((line.shape[0] - span, chans), jnp.float32)
            windows[0:segment, :] = jnp.zeros((segment, MAXS * chans), jnp.bfloat16)
            last = (bands + 1) * segment
            windows[last : last + segment, :] = jnp.zeros((segment, MAXS * chans), jnp.bfloat16)
            fill(0)

        @pl.when(band + 1 < bands)
        def _():
            fill(band + 1)

        start = pl.multiple_of(band * segment, segment)
        conv = jnp.dot(t_ref[0], windows[pl.ds(start, lanes), :], preferred_element_type=jnp.float32)
        conv = conv[:used]
        mixed_in = jnp.concatenate(
            [
                jnp.concatenate(
                    [
                        conv[k * longitudes : (k + 1) * longitudes, r * chans : (r + 1) * chans]
                        for k in range(filters)
                    ],
                    1,
                )
                for r in range(MAXS)
            ],
            0,
        ).astype(jnp.bfloat16)
        mixed = jnp.dot(mixed_in, w_ref[...], preferred_element_type=jnp.float32)
        mine_ref[0] = mixed[:longitudes]
        for r in range(1, MAXS):
            rest_ref[r - 1, 0] = mixed[r * longitudes : (r + 1) * longitudes].astype(jnp.bfloat16)

    whole = pl.BlockSpec((MAXS, bands, longitudes, chans), lambda i: (0, 0, 0, 0))
    return pl.pallas_call(
        body,
        grid=(bands,),
        in_specs=[
            pl.BlockSpec(memory_space=pltpu.SMEM),
            pl.BlockSpec((1, rows, lanes), lambda i: (i, 0, 0)),
            whole,
            whole,
            whole,
            pl.BlockSpec(weights.shape, lambda i: (0, 0)),
        ],
        out_specs=[
            pl.BlockSpec((1, longitudes, outs), lambda i: (i, 0, 0)),
            pl.BlockSpec((MAXS - 1, 1, longitudes, outs), lambda i: (0, i, 0, 0)),
        ],
        out_shape=[
            jax.ShapeDtypeStruct((bands, longitudes, outs), jnp.float32),
            jax.ShapeDtypeStruct((MAXS - 1, bands, longitudes, outs), jnp.bfloat16),
        ],
        scratch_shapes=[
            pltpu.VMEM((MAXS * longitudes + round_up(window, segment) + 2 * longitudes, chans), jnp.float32),
            pltpu.VMEM(((bands + 2) * segment, MAXS * chans), jnp.bfloat16),
        ],
        compiler_params=pltpu.CompilerParams(vmem_limit_bytes=VMEM),
        name="convolve_and_mix",
    )(place, matrices, *planes, weights)


def finish(mine, others):
    bands, longitudes, outs = mine.shape

    def body(mine_ref, a_ref, b_ref, c_ref, out_ref):
        total = mine_ref[...] + a_ref[...].astype(jnp.float32)
        total += b_ref[...].astype(jnp.float32) + c_ref[...].astype(jnp.float32)
        out_ref[...] = jax.nn.gelu(total).astype(jnp.bfloat16)

    block = pl.BlockSpec((2, longitudes, outs), lambda i: (i, 0, 0))
    return pl.pallas_call(
        body,
        grid=(bands // 2,),
        in_specs=[block] * MAXS,
        out_specs=block,
        out_shape=jax.ShapeDtypeStruct(mine.shape, jnp.bfloat16),
        compiler_params=pltpu.CompilerParams(vmem_limit_bytes=VMEM),
        name="finish",
    )(mine, *others)


def gather_weights(mixing, filters, channels):
    held, outs = mixing.shape
    chans = channels // MAXS
    devices = lax.axis_size("lon")
    groups = lax.axis_size("groups")
    lon = lax.axis_index("lon")
    place = lon % MAXS
    planes = devices // MAXS
    part = held // groups
    units = part // UNIT
    per_filter = channels // UNIT
    per_quarter = chans // UNIT
    plane_units = MAXS * held // UNIT
    fits = (
        groups == 2
        and planes == MAXS
        and part % UNIT == 0
        and (plane_units % per_filter) * MAXS % per_filter == 0
        and plane_units % per_filter == per_quarter
    )
    if not fits:
        whole = lax.all_gather(mixing, "lon", axis=0, tiled=True).reshape(filters, channels, outs)
        mine = lax.dynamic_slice_in_dim(whole, place * chans, chans, 1)
        return mine.reshape(filters * chans, outs)
    group = lax.axis_index("groups")
    plane = lon // MAXS
    rows = lax.dynamic_slice_in_dim(mixing, group * part, part, 0)[None]
    step = 1
    while step < planes:
        arrived = send(rows, "lon", lambda s, step=step: s ^ (step * MAXS))
        rows = jnp.concatenate([rows, arrived], 0)
        step *= 2
    rows = rows.reshape(planes, units, UNIT, outs)
    first = place * (held // UNIT) + group * units + jnp.arange(units)
    base = (first % per_filter) // per_quarter

    def for_quarter(quarter):
        entry = ((quarter - base) % MAXS) ^ plane
        picked = rows[0]
        for z in range(1, planes):
            picked = jnp.where((entry == z)[:, None, None], rows[z], picked)
        return picked

    pieces = [for_quarter(place)]
    for r in range(1, MAXS):
        pieces.append(send(for_quarter(place ^ r), "lon", lambda s, r=r: s ^ r))
    mine = jnp.stack(pieces)
    theirs = send(mine, "groups", lambda s: s ^ 1)
    mine = mine.reshape(MAXS * units, UNIT, outs)
    theirs = theirs.reshape(MAXS * units, UNIT, outs)
    wanted = jnp.arange(filters * per_quarter)
    source = wanted // per_quarter * per_filter + place * per_quarter + wanted % per_quarter
    device, index = source // (held // UNIT), source % (held // UNIT)
    position = ((device % MAXS) ^ place) * units + index % units
    swapped = (index // units) ^ group

    def body(position_ref, swapped_ref, mine_ref, theirs_ref, out_ref):
        for u in range(filters * per_quarter):
            at, other = position_ref[u], swapped_ref[u]
            value = jnp.where(other == 1, theirs_ref[at], mine_ref[at])
            out_ref[u * UNIT : (u + 1) * UNIT, :] = value

    return pl.pallas_call(
        body,
        in_specs=[pl.BlockSpec(memory_space=pltpu.SMEM)] * 2 + [pl.BlockSpec(memory_space=pltpu.VMEM)] * 2,
        out_specs=pl.BlockSpec(memory_space=pltpu.VMEM),
        out_shape=jax.ShapeDtypeStruct((filters * chans, outs), mixing.dtype),
        compiler_params=pltpu.CompilerParams(vmem_limit_bytes=VMEM),
        name="sort_weights",
    )(position.astype(jnp.int32), swapped.astype(jnp.int32), mine, theirs)


def on_device(inputs, support, basis_table, mixing):
    bands, longitudes, channels = inputs.shape
    filters = basis_table.shape[0]
    chans = channels // MAXS
    devices = lax.axis_size("lon")
    place = lax.axis_index("lon") % MAXS

    def quarter(r):
        return lax.dynamic_slice_in_dim(inputs, (place ^ r) * chans, chans, 2)

    pieces = [quarter(0)] + [send(quarter(r), "lon", lambda s, r=r: s ^ r) for r in range(1, MAXS)]
    own = jnp.stack(pieces)
    west = send(own, "lon", lambda s: (s + MAXS) % devices)
    east = send(own, "lon", lambda s: (s - MAXS) % devices)

    weights = gather_weights(mixing, filters, channels)
    segment = round_up((2 * MAXS + 1) * longitudes, 128)
    matrices = toeplitz(packed_basis(basis_table, support, longitudes, segment), longitudes)
    mine, rest = convolve_and_mix(
        place.reshape(1).astype(jnp.int32), matrices, (west, own, east), weights, filters
    )
    others = [send(rest[r - 1], "lon", lambda s, r=r: s ^ r) for r in range(1, MAXS)]
    return finish(mine, others)


def solution(mesh):
    placed = (P("groups", "lon", None), P("groups"), P(None, "groups", None, None), P("lon", None))
    return jax.shard_map(
        on_device, mesh=mesh, in_specs=placed, out_specs=P("groups", "lon", None), check_vma=False
    )
```

```python
import jax
import jax.numpy as jnp
from jax import lax
from jax.experimental import pallas as pl
from jax.experimental.pallas import tpu as pltpu
from jax.sharding import PartitionSpec as P

MAXS = 4
UNIT = 16
VMEM = 28 << 20


def send(value, axis, target_of):
    count = lax.axis_size(axis)
    return lax.ppermute(value, axis, [(s, target_of(s)) for s in range(count)])


def round_up(value, step):
    return -(-value // step) * step


def lay_out(pieces, first, last, ties):
    shape = (len(pieces), last - first, *pieces[0].shape[1:])

    def body(*refs):
        for n in range(len(pieces)):
            refs[-1][n] = refs[n][first:last]

    return pl.pallas_call(
        body,
        in_specs=[pl.BlockSpec(memory_space=pltpu.VMEM)] * len(pieces)
        + [pl.BlockSpec(memory_space=pl.ANY)] * len(ties),
        out_specs=pl.BlockSpec(memory_space=pltpu.VMEM),
        out_shape=jax.ShapeDtypeStruct(shape, pieces[0].dtype),
        compiler_params=pltpu.CompilerParams(vmem_limit_bytes=VMEM),
        name="lay_out",
    )(*pieces, *ties)


def packed_basis(basis_table, support, longitudes, segment):
    filters, bands, three, offsets = basis_table.shape
    distance = jnp.abs(jnp.arange(offsets) - MAXS * longitudes)
    within = distance[None, :] <= (support * longitudes)[:, None]
    rows = jnp.where(within[None, :, None, :], basis_table, jnp.zeros_like(basis_table))
    rows = jnp.pad(rows, ((0, 0), (0, 0), (0, 0), (0, segment - offsets)))
    rows = rows.transpose(1, 0, 2, 3).reshape(bands, filters, three * segment)
    return rows.astype(jnp.float32)


def fill_toeplitz(row_of, out_ref, filters, longitudes):
    rows, lanes = out_ref.shape

    def block(k):
        row = jnp.broadcast_to(row_of(k), (longitudes, lanes))
        return pltpu.roll(row, 0, 1, stride=1, stride_axis=0)

    for k in range(0, filters, 2):
        start = k * longitudes
        if k + 1 < filters:
            pair = jnp.concatenate([block(k), block(k + 1)], 0)
        else:
            tail = jnp.zeros((rows - start - longitudes, lanes), jnp.float32)
            pair = jnp.concatenate([block(k), tail], 0)
        out_ref[start : start + pair.shape[0], :] = pair.astype(jnp.bfloat16)


def convolve(place, packed, planes, first, bands):
    longitudes, chans = planes[0][0][1].shape[2:]
    count, filters, lanes = packed.shape
    rows = round_up(filters * longitudes, UNIT)
    segment = lanes // 3
    span = 3 * MAXS * longitudes
    step = round_up(longitudes, UNIT)
    low, high = max(first - 1, 0), min(first + count + 1, bands)
    arrays, found = [], [{}, {}, {}]
    for t in range(3):
        for start, array in planes[t]:
            for b in range(array.shape[1]):
                found[t][start + b] = (len(arrays), b)
            arrays.append(array)

    def body(place_ref, packed_ref, *refs):
        ins, (mixin, line, windows, toeplitz) = refs[: len(arrays)], refs[len(arrays) :]
        here = place_ref[0]
        line[:, span:, :] = jnp.zeros((2, line.shape[1] - span, chans), jnp.float32)
        for b in range(low, high):
            side = b % 2
            for t in range(3):
                which, at = found[t][b]
                for p in range(MAXS):
                    start = (t * MAXS + p) * longitudes
                    line[side, start : start + longitudes, :] = ins[which][p ^ here, at].astype(jnp.float32)
            start = (b - low) * segment
            for r in range(MAXS):
                begin = pl.multiple_of((r ^ here) * longitudes, 8)
                part = line[side, pl.ds(begin, segment), :].astype(jnp.bfloat16)
                windows[start : start + segment, r * chans : (r + 1) * chans] = part
        for c in range(count):
            i = first + c
            from_band, to_band = max(i - 1, 0), min(i + 2, bands)
            matrix = toeplitz.at[c % 2]
            fill_toeplitz(lambda k, c=c: packed_ref[c, k : k + 1, :], matrix, filters, longitudes)
            matrix = matrix[:, (from_band - i + 1) * segment : (to_band - i + 1) * segment]
            window = windows[(from_band - low) * segment : (to_band - low) * segment, :]
            conv = jnp.dot(matrix, window, preferred_element_type=jnp.float32)
            for r in range(MAXS):
                parts = [
                    conv[k * longitudes : (k + 1) * longitudes, r * chans : (r + 1) * chans]
                    for k in range(filters)
                ]
                part = jnp.concatenate(parts, 1)
                fill = jnp.zeros((step - longitudes, part.shape[1]), jnp.float32)
                start = (c * MAXS + r) * step
                mixin[start : start + step, :] = jnp.concatenate([part, fill], 0).astype(jnp.bfloat16)

    vmem = pl.BlockSpec(memory_space=pltpu.VMEM)
    return pl.pallas_call(
        body,
        in_specs=[pl.BlockSpec(memory_space=pltpu.SMEM)] + [vmem] * (1 + len(arrays)),
        out_specs=vmem,
        out_shape=jax.ShapeDtypeStruct((count * MAXS * step, filters * chans), jnp.bfloat16),
        scratch_shapes=[
            pltpu.VMEM((2, round_up((MAXS - 1) * longitudes + max(segment, span), 8), chans), jnp.float32),
            pltpu.VMEM(((high - low) * segment, MAXS * chans), jnp.bfloat16),
            pltpu.VMEM((2, rows, lanes), jnp.bfloat16),
        ],
        compiler_params=pltpu.CompilerParams(vmem_limit_bytes=VMEM),
        cost_estimate=pl.CostEstimate(
            flops=2 * count * rows * lanes * MAXS * chans, bytes_accessed=1, transcendentals=0
        ),
        name="convolve",
    )(place, packed, *arrays)


def mix(convolved, weights, longitudes):
    step = round_up(longitudes, UNIT)
    counts = [array.shape[0] // (MAXS * step) for array in convolved]
    outs = weights.shape[1]

    def body(w_ref, *refs):
        ins, (kept_ref, sent_ref) = refs[:-2], refs[-2:]
        first = 0
        for ref, count in zip(ins, counts):
            mixed = jnp.dot(ref[...], w_ref[...], preferred_element_type=jnp.float32)
            for c in range(count):
                for r in range(MAXS):
                    start = (c * MAXS + r) * step
                    value = mixed[start : start + longitudes]
                    if r % 2 == 0:
                        kept_ref[r // 2, first + c] = value
                    else:
                        sent_ref[r // 2, first + c] = value.astype(jnp.bfloat16)
            first += count

    vmem = pl.BlockSpec(memory_space=pltpu.VMEM)
    shape = (2, sum(counts), longitudes, outs)
    return pl.pallas_call(
        body,
        in_specs=[vmem] * (1 + len(convolved)),
        out_specs=[vmem, vmem],
        out_shape=[jax.ShapeDtypeStruct(shape, jnp.float32), jax.ShapeDtypeStruct(shape, jnp.bfloat16)],
        compiler_params=pltpu.CompilerParams(vmem_limit_bytes=VMEM),
        name="mix",
    )(weights, *convolved)


def finish(turned, sums, bands):
    longitudes, width = sums[0][1].shape[2:]

    def body(turned_ref, *refs):
        out_ref = refs[-1]
        reached = [0, 0]
        for n, (half, kept, _, _) in enumerate(sums):
            kept_ref, core_ref, across_ref = refs[3 * n : 3 * n + 3]
            column = pl.multiple_of((turned_ref[0] ^ half) * width, width)
            for band in range(kept.shape[1]):
                total = kept_ref[0, band] + core_ref[0, band].astype(jnp.float32)
                total += across_ref[band].astype(jnp.float32)
                out_ref[reached[half], :, pl.ds(column, width)] = jax.nn.gelu(total).astype(jnp.bfloat16)
                reached[half] += 1

    vmem = pl.BlockSpec(memory_space=pltpu.VMEM)
    return pl.pallas_call(
        body,
        in_specs=[pl.BlockSpec(memory_space=pltpu.SMEM)] + [vmem] * (3 * len(sums)),
        out_specs=vmem,
        out_shape=jax.ShapeDtypeStruct((bands, longitudes, 2 * width), jnp.bfloat16),
        compiler_params=pltpu.CompilerParams(vmem_limit_bytes=VMEM),
        name="finish",
    )(turned, *(array for entry in sums for array in entry[1:]))


def gather_weights(mixing, filters, channels):
    held, outs = mixing.shape
    chans = channels // MAXS
    width = outs // 2
    devices = lax.axis_size("lon")
    groups = lax.axis_size("groups")
    lon = lax.axis_index("lon")
    place = lon % MAXS
    planes = devices // MAXS
    units = held // UNIT
    per_filter = channels // UNIT
    per_quarter = chans // UNIT
    fits = (
        groups == 2
        and planes == MAXS
        and held % UNIT == 0
        and (MAXS * units) % per_filter == per_quarter
    )
    if not fits:
        whole = lax.all_gather(mixing, "lon", axis=0, tiled=True).reshape(filters, channels, outs)
        mine = lax.dynamic_slice_in_dim(whole, place * chans, chans, 1).reshape(filters * chans, outs)
        return (), lambda *_: (mine[:, :width], mine[:, width:], jnp.int32(0))
    group = lax.axis_index("groups")
    plane = lon // MAXS
    rows = lax.dynamic_slice_in_dim(mixing, group * width, width, 1)
    far = send(rows, "lon", lambda s: s ^ (2 * MAXS))
    near = send(rows, "lon", lambda s: s ^ MAXS)
    rows = jnp.stack([rows, near, far, send(far, "lon", lambda s: s ^ MAXS)])
    rows = rows.reshape(planes, units, UNIT, width)
    base = (place * units + jnp.arange(units)) % per_filter // per_quarter

    def for_quarter(quarter):
        entry = ((quarter - base) % MAXS) ^ plane
        picked = rows[0]
        for z in range(1, planes):
            picked = jnp.where((entry == z)[:, None, None], rows[z], picked)
        return picked

    pieces = {0: for_quarter(place)}
    for r in (3, 2, 1):
        pieces[r] = send(for_quarter(place ^ r), "lon", lambda s, r=r: s ^ r)
    def sort(*ties):
        mine = jnp.concatenate([pieces[r] for r in range(MAXS)])
        count = filters * per_quarter
        wanted = jnp.arange(count)
        source = wanted // per_quarter * per_filter + place * per_quarter + wanted % per_quarter
        position = (source // units % MAXS ^ place) * units + source % units

        def body(position_ref, mine_ref, *refs):
            for u in range(count):
                refs[-1][u * UNIT : (u + 1) * UNIT, :] = mine_ref[position_ref[u]]

        ours = pl.pallas_call(
            body,
            in_specs=[pl.BlockSpec(memory_space=pltpu.SMEM), pl.BlockSpec(memory_space=pltpu.VMEM)]
            + [pl.BlockSpec(memory_space=pl.ANY)] * len(ties),
            out_specs=pl.BlockSpec(memory_space=pltpu.VMEM),
            out_shape=jax.ShapeDtypeStruct((filters * chans, width), mixing.dtype),
            compiler_params=pltpu.CompilerParams(vmem_limit_bytes=VMEM),
            name="sort_weights",
        )(position.astype(jnp.int32), mine, *ties)
        return ours, send(ours, "groups", lambda s: s ^ 1), group

    return (pieces[1], pieces[2], pieces[3]), sort


def on_device(inputs, support, basis_table, mixing):
    bands, longitudes, channels = inputs.shape
    filters = basis_table.shape[0]
    chans = channels // MAXS
    devices = lax.axis_size("lon")
    place = lax.axis_index("lon") % MAXS
    segment = round_up((2 * MAXS + 1) * longitudes, 128)
    packed = packed_basis(basis_table, support, longitudes, segment)
    cuts = ((0, 4), (4, 8))

    def quarter(r):
        return lax.dynamic_slice_in_dim(inputs, (place ^ r) * chans, chans, 2)

    pieces = {0: quarter(0)}
    for r in (3, 2, 1):
        pieces[r] = send(quarter(r), "lon", lambda s, r=r: s ^ r)
    arrived, sort = gather_weights(mixing, filters, channels)
    planes = [[], [], []]
    reached = 0
    for index, (first, last) in enumerate(cuts):
        until = min(last + 1, bands)
        ties = list(arrived) if index else []
        own = lay_out([pieces[r] for r in range(MAXS)], reached, until, ties)
        west = send(own, "lon", lambda s: (s + MAXS) % devices)
        east = send(own, "lon", lambda s: (s - MAXS) % devices)
        for held, array in zip(planes, (west, own, east)):
            held.append((reached, array))
        reached = until
    ours, theirs, turned = sort()

    here = place.reshape(1).astype(jnp.int32)
    convolved = []
    for index, (first, last) in enumerate(cuts):
        low, high = max(first - 1, 0), min(last + 1, bands)
        needed = [[(s, a) for s, a in held if s < high and s + a.shape[1] > low] for held in planes]
        convolved.append(convolve(here, packed[first:last], needed, first, bands))

    def summed(half, arrays, weights):
        kept, sent = mix(arrays, weights, longitudes)
        core = send(sent, "lon", lambda s: s ^ 1)
        across = (kept[1] + core[1].astype(jnp.float32)).astype(jnp.bfloat16)
        return half, kept, core, send(across, "lon", lambda s: s ^ 2)

    sums = [summed(0, [array], ours) for array in convolved] + [summed(1, convolved, theirs)]
    return finish(turned.reshape(1).astype(jnp.int32), sums, bands)


def solution(mesh):
    placed = (P("groups", "lon", None), P("groups"), P(None, "groups", None, None), P("lon", None))
    return jax.shard_map(
        on_device, mesh=mesh, in_specs=placed, out_specs=P("groups", "lon", None), check_vma=False
    )
```

```python
import jax
import jax.numpy as jnp
from jax import lax
from jax.experimental import pallas as pl
from jax.experimental.pallas import tpu as pltpu
from jax.sharding import PartitionSpec as P

MAXS = 4
UNIT = 16
VMEM = 28 << 20
WORK = 4_500_000_000


def send(value, axis, target_of):
    count = lax.axis_size(axis)
    return lax.ppermute(value, axis, [(s, target_of(s)) for s in range(count)])


def round_up(value, step):
    return -(-value // step) * step


def lay_out(pieces, first, last, ties):
    shape = (len(pieces), last - first, *pieces[0].shape[1:])

    def body(*refs):
        for n in range(len(pieces)):
            refs[-1][n] = refs[n][first:last]

    return pl.pallas_call(
        body,
        in_specs=[pl.BlockSpec(memory_space=pltpu.VMEM)] * len(pieces)
        + [pl.BlockSpec(memory_space=pl.ANY)] * len(ties),
        out_specs=pl.BlockSpec(memory_space=pltpu.VMEM),
        out_shape=jax.ShapeDtypeStruct(shape, pieces[0].dtype),
        compiler_params=pltpu.CompilerParams(vmem_limit_bytes=VMEM),
        name="lay_out",
    )(*pieces, *ties)


def packed_basis(basis_table, support, longitudes, segment):
    filters, bands, three, offsets = basis_table.shape
    distance = jnp.abs(jnp.arange(offsets) - MAXS * longitudes)
    within = distance[None, :] <= (support * longitudes)[:, None]
    rows = jnp.where(within[None, :, None, :], basis_table, jnp.zeros_like(basis_table))
    rows = jnp.pad(rows, ((0, 0), (0, 0), (0, 0), (0, segment - offsets)))
    rows = rows.transpose(1, 0, 2, 3).reshape(bands, filters, three * segment)
    return rows.astype(jnp.float32)


def fill_toeplitz(row_of, out_ref, filters, longitudes):
    rows, lanes = out_ref.shape

    def block(k):
        row = jnp.broadcast_to(row_of(k), (longitudes, lanes))
        return pltpu.roll(row, 0, 1, stride=1, stride_axis=0)

    for k in range(0, filters, 2):
        start = k * longitudes
        if k + 1 < filters:
            pair = jnp.concatenate([block(k), block(k + 1)], 0)
        else:
            tail = jnp.zeros((rows - start - longitudes, lanes), jnp.float32)
            pair = jnp.concatenate([block(k), tail], 0)
        out_ref[start : start + pair.shape[0], :] = pair.astype(jnp.bfloat16)


def convolve(place, packed, planes, slots, first, bands, ties):
    longitudes, chans = planes[0][0][1].shape[2:]
    count, filters, lanes = packed.shape
    rows = round_up(filters * longitudes, UNIT)
    segment = lanes // 3
    span = 3 * MAXS * longitudes
    low, high = max(first - 1, 0), min(first + count + 1, bands)
    arrays, found = [], [{}, {}, {}]
    for t in range(3):
        for start, array in planes[t]:
            for b in range(array.shape[1]):
                found[t][start + b] = (len(arrays), b)
            arrays.append(array)

    def body(place_ref, packed_ref, *refs):
        ins, (mixin, line, windows, toeplitz) = refs[: len(arrays)], refs[len(arrays) + len(ties) :]
        here = place_ref[0]
        line[:, span:, :] = jnp.zeros((2, line.shape[1] - span, chans), jnp.float32)
        for b in range(low, high):
            side = b % 2
            for t in range(3):
                which, at = found[t][b]
                for p in range(MAXS):
                    start = (t * MAXS + p) * longitudes
                    line[side, start : start + longitudes, :] = ins[which][p ^ here, at].astype(jnp.float32)
            start = (b - low) * segment
            for n, r in enumerate(slots):
                begin = pl.multiple_of((r ^ here) * longitudes, 8)
                part = line[side, pl.ds(begin, segment), :].astype(jnp.bfloat16)
                windows[start : start + segment, n * chans : (n + 1) * chans] = part
        for c in range(count):
            i = first + c
            from_band, to_band = max(i - 1, 0), min(i + 2, bands)
            matrix = toeplitz.at[c % 2]
            fill_toeplitz(lambda k, c=c: packed_ref[c, k : k + 1, :], matrix, filters, longitudes)
            matrix = matrix[:, (from_band - i + 1) * segment : (to_band - i + 1) * segment]
            window = windows[(from_band - low) * segment : (to_band - low) * segment, :]
            conv = jnp.dot(matrix, window, preferred_element_type=jnp.float32)
            for pair in range(0, len(slots), 2):
                rows_of = []
                for n in (pair, pair + 1):
                    parts = [
                        conv[k * longitudes : (k + 1) * longitudes, n * chans : (n + 1) * chans]
                        for k in range(filters)
                    ]
                    rows_of.append(jnp.concatenate(parts, 1))
                start = (pair // 2 * count + c) * 2 * longitudes
                mixin[start : start + 2 * longitudes, :] = jnp.concatenate(rows_of, 0).astype(jnp.bfloat16)

    vmem = pl.BlockSpec(memory_space=pltpu.VMEM)
    return pl.pallas_call(
        body,
        in_specs=[pl.BlockSpec(memory_space=pltpu.SMEM)]
        + [vmem] * (1 + len(arrays))
        + [pl.BlockSpec(memory_space=pl.ANY)] * len(ties),
        out_specs=vmem,
        out_shape=jax.ShapeDtypeStruct((count * len(slots) * longitudes, filters * chans), jnp.bfloat16),
        scratch_shapes=[
            pltpu.VMEM((2, round_up((MAXS - 1) * longitudes + max(segment, span), 8), chans), jnp.float32),
            pltpu.VMEM(((high - low) * segment, len(slots) * chans), jnp.bfloat16),
            pltpu.VMEM((2, rows, lanes), jnp.bfloat16),
        ],
        compiler_params=pltpu.CompilerParams(vmem_limit_bytes=VMEM),
        cost_estimate=pl.CostEstimate(
            flops=WORK, bytes_accessed=1, transcendentals=0
        ),
        name="convolve",
    )(place, packed, *arrays, *ties)


def mix(convolved, slots, weights, longitudes, ties):
    pair = convolved.shape[0] // (MAXS // 2)
    count = pair // (2 * longitudes)
    half = len(slots) // 2
    width = weights[0].shape[1]
    begin = slots[0] // 2 * pair

    def body(conv_ref, *refs):
        kept_ref, sent_ref = refs[-2:]
        block = conv_ref[begin : begin + half * pair, :]
        for n in range(len(weights)):
            mixed = jnp.dot(block, refs[n][...], preferred_element_type=jnp.float32)
            for h in range(half):
                for c in range(count):
                    start = h * pair + c * 2 * longitudes
                    value = mixed[start : start + longitudes]
                    kept_ref[h, c, :, n * width : (n + 1) * width] = value
                    value = mixed[start + longitudes : start + 2 * longitudes].astype(jnp.bfloat16)
                    sent_ref[h, c, :, n * width : (n + 1) * width] = value

    vmem = pl.BlockSpec(memory_space=pltpu.VMEM)
    shape = (half, count, longitudes, len(weights) * width)
    return pl.pallas_call(
        body,
        in_specs=[vmem] * (1 + len(weights)) + [pl.BlockSpec(memory_space=pl.ANY)] * len(ties),
        out_specs=[vmem, vmem],
        out_shape=[jax.ShapeDtypeStruct(shape, jnp.float32), jax.ShapeDtypeStruct(shape, jnp.bfloat16)],
        compiler_params=pltpu.CompilerParams(vmem_limit_bytes=VMEM),
        name="mix",
    )(convolved, *weights, *ties)


def finish(turned, sums, width, bands):
    longitudes = sums[0][2].shape[2]

    def body(turned_ref, *refs):
        out_ref = refs[-1]
        for n, (first, halves, kept, _, _) in enumerate(sums):
            kept_ref, core_ref, across_ref = refs[3 * n : 3 * n + 3]
            for m, half in enumerate(halves):
                column = pl.multiple_of((turned_ref[0] ^ half) * width, width)
                from_ = slice(m * width, (m + 1) * width)
                for band in range(kept.shape[1]):
                    total = kept_ref[0, band, :, from_] + core_ref[0, band, :, from_].astype(jnp.float32)
                    total += across_ref[band, :, from_].astype(jnp.float32)
                    out_ref[first + band, :, pl.ds(column, width)] = jax.nn.gelu(total).astype(jnp.bfloat16)

    vmem = pl.BlockSpec(memory_space=pltpu.VMEM)
    return pl.pallas_call(
        body,
        in_specs=[pl.BlockSpec(memory_space=pltpu.SMEM)] + [vmem] * (3 * len(sums)),
        out_specs=vmem,
        out_shape=jax.ShapeDtypeStruct((bands, longitudes, 2 * width), jnp.bfloat16),
        compiler_params=pltpu.CompilerParams(vmem_limit_bytes=VMEM),
        name="finish",
    )(turned, *(array for entry in sums for array in entry[2:]))


def gather_weights(mixing, filters, channels):
    held, outs = mixing.shape
    chans = channels // MAXS
    width = outs // 2
    devices = lax.axis_size("lon")
    groups = lax.axis_size("groups")
    lon = lax.axis_index("lon")
    place = lon % MAXS
    planes = devices // MAXS
    units = held // UNIT
    per_filter = channels // UNIT
    per_quarter = chans // UNIT
    fits = (
        groups == 2
        and planes == MAXS
        and held % UNIT == 0
        and (MAXS * units) % per_filter == per_quarter
    )
    if not fits:
        whole = lax.all_gather(mixing, "lon", axis=0, tiled=True).reshape(filters, channels, outs)
        mine = lax.dynamic_slice_in_dim(whole, place * chans, chans, 1).reshape(filters * chans, outs)
        return (), lambda *_: (mine[:, :width], mine[:, width:], jnp.int32(0))
    group = lax.axis_index("groups")
    plane = lon // MAXS
    rows = lax.dynamic_slice_in_dim(mixing, group * width, width, 1)
    far = send(rows, "lon", lambda s: s ^ (2 * MAXS))
    near = send(rows, "lon", lambda s: s ^ MAXS)
    rows = jnp.stack([rows, near, far, send(far, "lon", lambda s: s ^ MAXS)])
    rows = rows.reshape(planes, units, UNIT, width)
    base = (place * units + jnp.arange(units)) % per_filter // per_quarter

    def for_quarter(quarter):
        entry = ((quarter - base) % MAXS) ^ plane
        picked = rows[0]
        for z in range(1, planes):
            picked = jnp.where((entry == z)[:, None, None], rows[z], picked)
        return picked

    pieces = {0: for_quarter(place)}
    for r in (3, 2, 1):
        pieces[r] = send(for_quarter(place ^ r), "lon", lambda s, r=r: s ^ r)
    def sort(*ties):
        mine = jnp.concatenate([pieces[r] for r in range(MAXS)])
        count = filters * per_quarter
        wanted = jnp.arange(count)
        source = wanted // per_quarter * per_filter + place * per_quarter + wanted % per_quarter
        position = (source // units % MAXS ^ place) * units + source % units

        def body(position_ref, mine_ref, *refs):
            for u in range(count):
                refs[-1][u * UNIT : (u + 1) * UNIT, :] = mine_ref[position_ref[u]]

        ours = pl.pallas_call(
            body,
            in_specs=[pl.BlockSpec(memory_space=pltpu.SMEM), pl.BlockSpec(memory_space=pltpu.VMEM)]
            + [pl.BlockSpec(memory_space=pl.ANY)] * len(ties),
            out_specs=pl.BlockSpec(memory_space=pltpu.VMEM),
            out_shape=jax.ShapeDtypeStruct((filters * chans, width), mixing.dtype),
            compiler_params=pltpu.CompilerParams(vmem_limit_bytes=VMEM),
            name="sort_weights",
        )(position.astype(jnp.int32), mine, *ties)
        return ours, send(ours, "groups", lambda s: s ^ 1), group

    return (pieces[1], pieces[2], pieces[3]), sort


def on_device(inputs, support, basis_table, mixing):
    bands, longitudes, channels = inputs.shape
    filters = basis_table.shape[0]
    chans = channels // MAXS
    devices = lax.axis_size("lon")
    place = lax.axis_index("lon") % MAXS
    segment = round_up((2 * MAXS + 1) * longitudes, 128)
    packed = packed_basis(basis_table, support, longitudes, segment)
    cuts = ((0, 6), (6, 8))

    def quarter(r):
        return lax.dynamic_slice_in_dim(inputs, (place ^ r) * chans, chans, 2)

    pieces = {0: quarter(0)}
    for r in (3, 2, 1):
        pieces[r] = send(quarter(r), "lon", lambda s, r=r: s ^ r)
    arrived, sort = gather_weights(mixing, filters, channels)
    planes = [[], [], []]
    reached = 0
    for index, (first, last) in enumerate(cuts):
        until = min(last + 1, bands)
        ties = list(arrived) if index else []
        own = lay_out([pieces[r] for r in range(MAXS)], reached, until, ties)
        west = send(own, "lon", lambda s: (s + MAXS) % devices)
        east = send(own, "lon", lambda s: (s - MAXS) % devices)
        for held, array in zip(planes, (west, own, east)):
            held.append((reached, array))
        reached = until
    ours, theirs, turned = sort()

    here = place.reshape(1).astype(jnp.int32)

    def convolved(index, slots, ties):
        first, last = cuts[index]
        low, high = max(first - 1, 0), min(last + 1, bands)
        needed = [[(s, a) for s, a in held if s < high and s + a.shape[1] > low] for held in planes]
        return convolve(here, packed[first:last], needed, slots, first, bands, ties)

    def over_core(sent):
        return send(sent, "lon", lambda s: s ^ 1)

    def added(kept, core):
        return (kept + core.astype(jnp.float32)).astype(jnp.bfloat16)

    def over_y(value):
        return send(value, "lon", lambda s: s ^ 2)

    every = tuple(range(MAXS))
    sums = []
    conv0 = convolved(0, every, [])
    kept_a, sent_a = mix(conv0, every, [ours], longitudes, [planes[0][1][1], planes[2][1][1]])
    core_a = over_core(sent_a)
    part_a = added(kept_a[1], core_a[1])
    across_a = over_y(part_a)
    sums.append((cuts[0][0], (0,), kept_a, core_a, across_a))
    kept_b, sent_b = mix(conv0, every, [theirs], longitudes, [])
    core_b = over_core(sent_b)
    part_b = added(kept_b[1], core_b[1])
    across_b = over_y(part_b)
    sums.append((cuts[0][0], (1,), kept_b, core_b, across_b))
    conv1 = convolved(1, every, [])
    kept, sent = mix(conv1, every, [ours, theirs], longitudes, [across_a])
    core = over_core(sent)
    sums.append((cuts[1][0], (0, 1), kept, core, over_y(added(kept[1], core[1]))))
    return finish(turned.reshape(1).astype(jnp.int32), sums, ours.shape[1], bands)


def solution(mesh):
    placed = (P("groups", "lon", None), P("groups"), P(None, "groups", None, None), P("lon", None))
    return jax.shard_map(
        on_device, mesh=mesh, in_specs=placed, out_specs=P("groups", "lon", None), check_vma=False
    )
```

```python
import jax
import jax.numpy as jnp
from jax import lax
from jax.experimental import pallas as pl
from jax.experimental.pallas import tpu as pltpu
from jax.sharding import PartitionSpec as P

MAXS = 4
UNIT = 16
VMEM = 28 << 20
WORK = 9_000_000_000


def send(value, axis, target_of):
    count = lax.axis_size(axis)
    return lax.ppermute(value, axis, [(s, target_of(s)) for s in range(count)])


def round_up(value, step):
    return -(-value // step) * step


def lay_out(pieces, first, last, ties):
    shape = (len(pieces), last - first, *pieces[0].shape[1:])

    def body(*refs):
        for n in range(len(pieces)):
            refs[-1][n] = refs[n][first:last]

    return pl.pallas_call(
        body,
        in_specs=[pl.BlockSpec(memory_space=pltpu.VMEM)] * len(pieces)
        + [pl.BlockSpec(memory_space=pl.ANY)] * len(ties),
        out_specs=pl.BlockSpec(memory_space=pltpu.VMEM),
        out_shape=jax.ShapeDtypeStruct(shape, pieces[0].dtype),
        compiler_params=pltpu.CompilerParams(vmem_limit_bytes=VMEM),
        name="lay_out",
    )(*pieces, *ties)


def packed_basis(basis_table, support, longitudes, segment):
    filters, bands, three, offsets = basis_table.shape
    distance = jnp.abs(jnp.arange(offsets) - MAXS * longitudes)
    within = distance[None, :] <= (support * longitudes)[:, None]
    rows = jnp.where(within[None, :, None, :], basis_table, jnp.zeros_like(basis_table))
    rows = jnp.pad(rows, ((0, 0), (0, 0), (0, 0), (0, segment - offsets)))
    rows = rows.transpose(1, 0, 2, 3).reshape(bands, filters, three * segment)
    return rows.astype(jnp.float32)


def fill_toeplitz(row_of, out_ref, filters, longitudes):
    rows, lanes = out_ref.shape

    def block(k):
        row = jnp.broadcast_to(row_of(k), (longitudes, lanes))
        return pltpu.roll(row, 0, 1, stride=1, stride_axis=0)

    for k in range(0, filters, 2):
        start = k * longitudes
        if k + 1 < filters:
            pair = jnp.concatenate([block(k), block(k + 1)], 0)
        else:
            tail = jnp.zeros((rows - start - longitudes, lanes), jnp.float32)
            pair = jnp.concatenate([block(k), tail], 0)
        out_ref[start : start + pair.shape[0], :] = pair.astype(jnp.bfloat16)


def convolve(place, packed, planes, slots, first, bands, ties):
    longitudes, chans = planes[0][0][1].shape[2:]
    count, filters, lanes = packed.shape
    rows = round_up(filters * longitudes, UNIT)
    segment = lanes // 3
    span = 3 * MAXS * longitudes
    low, high = max(first - 1, 0), min(first + count + 1, bands)
    arrays, found = [], [{}, {}, {}]
    for t in range(3):
        for start, array in planes[t]:
            for b in range(array.shape[1]):
                found[t][start + b] = (len(arrays), b)
            arrays.append(array)

    def body(place_ref, packed_ref, *refs):
        ins, (mixin, line, windows, toeplitz) = refs[: len(arrays)], refs[len(arrays) + len(ties) :]
        here = place_ref[0]
        line[:, span:, :] = jnp.zeros((2, line.shape[1] - span, chans), jnp.float32)
        for b in range(low, high):
            side = b % 2
            for t in range(3):
                which, at = found[t][b]
                for p in range(MAXS):
                    start = (t * MAXS + p) * longitudes
                    line[side, start : start + longitudes, :] = ins[which][p ^ here, at].astype(jnp.float32)
            start = (b - low) * segment
            for n, r in enumerate(slots):
                begin = pl.multiple_of((r ^ here) * longitudes, 8)
                part = line[side, pl.ds(begin, segment), :].astype(jnp.bfloat16)
                windows[start : start + segment, n * chans : (n + 1) * chans] = part
        for c in range(count):
            i = first + c
            from_band, to_band = max(i - 1, 0), min(i + 2, bands)
            matrix = toeplitz.at[c % 2]
            fill_toeplitz(lambda k, c=c: packed_ref[c, k : k + 1, :], matrix, filters, longitudes)
            matrix = matrix[:, (from_band - i + 1) * segment : (to_band - i + 1) * segment]
            window = windows[(from_band - low) * segment : (to_band - low) * segment, :]
            conv = jnp.dot(matrix, window, preferred_element_type=jnp.float32)
            for pair in range(0, len(slots), 2):
                rows_of = []
                for n in (pair, pair + 1):
                    parts = [
                        conv[k * longitudes : (k + 1) * longitudes, n * chans : (n + 1) * chans]
                        for k in range(filters)
                    ]
                    rows_of.append(jnp.concatenate(parts, 1))
                start = (pair // 2 * count + c) * 2 * longitudes
                mixin[start : start + 2 * longitudes, :] = jnp.concatenate(rows_of, 0).astype(jnp.bfloat16)

    vmem = pl.BlockSpec(memory_space=pltpu.VMEM)
    return pl.pallas_call(
        body,
        in_specs=[pl.BlockSpec(memory_space=pltpu.SMEM)]
        + [vmem] * (1 + len(arrays))
        + [pl.BlockSpec(memory_space=pl.ANY)] * len(ties),
        out_specs=vmem,
        out_shape=jax.ShapeDtypeStruct((count * len(slots) * longitudes, filters * chans), jnp.bfloat16),
        scratch_shapes=[
            pltpu.VMEM((2, round_up((MAXS - 1) * longitudes + max(segment, span), 8), chans), jnp.float32),
            pltpu.VMEM(((high - low) * segment, len(slots) * chans), jnp.bfloat16),
            pltpu.VMEM((2, rows, lanes), jnp.bfloat16),
        ],
        compiler_params=pltpu.CompilerParams(vmem_limit_bytes=VMEM),
        cost_estimate=pl.CostEstimate(
            flops=WORK, bytes_accessed=1, transcendentals=0
        ),
        name="convolve",
    )(place, packed, *arrays, *ties)


def mix(convolved, slots, weights, longitudes, ties):
    pair = convolved.shape[0] // (MAXS // 2)
    count = pair // (2 * longitudes)
    half = len(slots) // 2
    width = weights[0].shape[1]
    begin = slots[0] // 2 * pair

    def body(conv_ref, *refs):
        kept_ref, sent_ref = refs[-2:]
        block = conv_ref[begin : begin + half * pair, :]
        for n in range(len(weights)):
            mixed = jnp.dot(block, refs[n][...], preferred_element_type=jnp.float32)
            for h in range(half):
                for c in range(count):
                    start = h * pair + c * 2 * longitudes
                    value = mixed[start : start + longitudes]
                    kept_ref[h, c, :, n * width : (n + 1) * width] = value
                    value = mixed[start + longitudes : start + 2 * longitudes].astype(jnp.bfloat16)
                    sent_ref[h, c, :, n * width : (n + 1) * width] = value

    vmem = pl.BlockSpec(memory_space=pltpu.VMEM)
    shape = (half, count, longitudes, len(weights) * width)
    return pl.pallas_call(
        body,
        in_specs=[vmem] * (1 + len(weights)) + [pl.BlockSpec(memory_space=pl.ANY)] * len(ties),
        out_specs=[vmem, vmem],
        out_shape=[jax.ShapeDtypeStruct(shape, jnp.float32), jax.ShapeDtypeStruct(shape, jnp.bfloat16)],
        compiler_params=pltpu.CompilerParams(vmem_limit_bytes=VMEM),
        name="mix",
    )(convolved, *weights, *ties)


def gelu_of(kept, core, across):
    def body(kept_ref, core_ref, across_ref, out_ref):
        total = kept_ref[0] + core_ref[0].astype(jnp.float32) + across_ref[...].astype(jnp.float32)
        out_ref[...] = jax.nn.gelu(total).astype(jnp.bfloat16)

    vmem = pl.BlockSpec(memory_space=pltpu.VMEM)
    return pl.pallas_call(
        body,
        in_specs=[vmem] * 3,
        out_specs=vmem,
        out_shape=jax.ShapeDtypeStruct(across.shape, jnp.bfloat16),
        compiler_params=pltpu.CompilerParams(vmem_limit_bytes=VMEM),
        name="gelu_of",
    )(kept, core, across)


def finish(turned, early, sums, width, bands):
    longitudes = sums[0][2].shape[2]
    ready = early.shape[0]

    def body(turned_ref, early_ref, *refs):
        out_ref, held, sems = refs[-3:]
        for band in range(bands):
            if band < ready:
                column = pl.multiple_of(turned_ref[0] * width, width)
                held[band, :, pl.ds(column, width)] = early_ref[band]
            for n, (first, halves, kept, _, _) in enumerate(sums):
                at = band - first
                if not 0 <= at < kept.shape[1]:
                    continue
                kept_ref, core_ref, across_ref = refs[3 * n : 3 * n + 3]
                for m, half in enumerate(halves):
                    column = pl.multiple_of((turned_ref[0] ^ half) * width, width)
                    from_ = slice(m * width, (m + 1) * width)
                    total = kept_ref[0, at, :, from_] + core_ref[0, at, :, from_].astype(jnp.float32)
                    total += across_ref[at, :, from_].astype(jnp.float32)
                    held[band, :, pl.ds(column, width)] = jax.nn.gelu(total).astype(jnp.bfloat16)
            pltpu.make_async_copy(held.at[band], out_ref.at[band], sems.at[band]).start()
        for band in range(bands):
            pltpu.make_async_copy(held.at[band], out_ref.at[band], sems.at[band]).wait()

    vmem = pl.BlockSpec(memory_space=pltpu.VMEM)
    return pl.pallas_call(
        body,
        in_specs=[pl.BlockSpec(memory_space=pltpu.SMEM)] + [vmem] * (1 + 3 * len(sums)),
        out_specs=pl.BlockSpec(memory_space=pl.ANY),
        out_shape=jax.ShapeDtypeStruct((bands, longitudes, 2 * width), jnp.bfloat16),
        scratch_shapes=[
            pltpu.VMEM((bands, longitudes, 2 * width), jnp.bfloat16),
            pltpu.SemaphoreType.DMA((bands,)),
        ],
        compiler_params=pltpu.CompilerParams(vmem_limit_bytes=VMEM),
        name="finish",
    )(turned, early, *(array for entry in sums for array in entry[2:]))


def gather_weights(mixing, filters, channels):
    held, outs = mixing.shape
    chans = channels // MAXS
    width = outs // 2
    devices = lax.axis_size("lon")
    groups = lax.axis_size("groups")
    lon = lax.axis_index("lon")
    place = lon % MAXS
    planes = devices // MAXS
    units = held // UNIT
    per_filter = channels // UNIT
    per_quarter = chans // UNIT
    fits = (
        groups == 2
        and planes == MAXS
        and held % UNIT == 0
        and (MAXS * units) % per_filter == per_quarter
    )
    if not fits:
        whole = lax.all_gather(mixing, "lon", axis=0, tiled=True).reshape(filters, channels, outs)
        mine = lax.dynamic_slice_in_dim(whole, place * chans, chans, 1).reshape(filters * chans, outs)
        return (), lambda *_: (mine[:, :width], mine[:, width:], jnp.int32(0))
    group = lax.axis_index("groups")
    plane = lon // MAXS
    rows = lax.dynamic_slice_in_dim(mixing, group * width, width, 1)
    far = send(rows, "lon", lambda s: s ^ (2 * MAXS))
    near = send(rows, "lon", lambda s: s ^ MAXS)
    rows = jnp.stack([rows, near, far, send(far, "lon", lambda s: s ^ MAXS)])
    rows = rows.reshape(planes, units, UNIT, width)
    base = (place * units + jnp.arange(units)) % per_filter // per_quarter

    def for_quarter(quarter):
        entry = ((quarter - base) % MAXS) ^ plane
        picked = rows[0]
        for z in range(1, planes):
            picked = jnp.where((entry == z)[:, None, None], rows[z], picked)
        return picked

    pieces = {0: for_quarter(place)}
    for r in (3, 2, 1):
        pieces[r] = send(for_quarter(place ^ r), "lon", lambda s, r=r: s ^ r)
    def sort(*ties):
        mine = jnp.concatenate([pieces[r] for r in range(MAXS)])
        count = filters * per_quarter
        wanted = jnp.arange(count)
        source = wanted // per_quarter * per_filter + place * per_quarter + wanted % per_quarter
        position = (source // units % MAXS ^ place) * units + source % units

        def body(position_ref, mine_ref, *refs):
            for u in range(count):
                refs[-1][u * UNIT : (u + 1) * UNIT, :] = mine_ref[position_ref[u]]

        ours = pl.pallas_call(
            body,
            in_specs=[pl.BlockSpec(memory_space=pltpu.SMEM), pl.BlockSpec(memory_space=pltpu.VMEM)]
            + [pl.BlockSpec(memory_space=pl.ANY)] * len(ties),
            out_specs=pl.BlockSpec(memory_space=pltpu.VMEM),
            out_shape=jax.ShapeDtypeStruct((filters * chans, width), mixing.dtype),
            compiler_params=pltpu.CompilerParams(vmem_limit_bytes=VMEM),
            name="sort_weights",
        )(position.astype(jnp.int32), mine, *ties)
        return ours, send(ours, "groups", lambda s: s ^ 1), group

    return (pieces[1], pieces[2], pieces[3]), sort


def on_device(inputs, support, basis_table, mixing):
    bands, longitudes, channels = inputs.shape
    filters = basis_table.shape[0]
    chans = channels // MAXS
    devices = lax.axis_size("lon")
    place = lax.axis_index("lon") % MAXS
    segment = round_up((2 * MAXS + 1) * longitudes, 128)
    packed = packed_basis(basis_table, support, longitudes, segment)
    cuts = ((0, 6), (6, 8))

    def quarter(r):
        return lax.dynamic_slice_in_dim(inputs, (place ^ r) * chans, chans, 2)

    pieces = {0: quarter(0)}
    for r in (3, 2, 1):
        pieces[r] = send(quarter(r), "lon", lambda s, r=r: s ^ r)
    arrived, sort = gather_weights(mixing, filters, channels)
    planes = [[], [], []]
    reached = 0
    for index, (first, last) in enumerate(cuts):
        until = min(last + 1, bands)
        ties = list(arrived) if index else []
        own = lay_out([pieces[r] for r in range(MAXS)], reached, until, ties)
        west = send(own, "lon", lambda s: (s + MAXS) % devices)
        east = send(own, "lon", lambda s: (s - MAXS) % devices)
        for held, array in zip(planes, (west, own, east)):
            held.append((reached, array))
        reached = until
    ours, theirs, turned = sort()

    here = place.reshape(1).astype(jnp.int32)

    def convolved(index, slots, ties):
        first, last = cuts[index]
        low, high = max(first - 1, 0), min(last + 1, bands)
        needed = [[(s, a) for s, a in held if s < high and s + a.shape[1] > low] for held in planes]
        return convolve(here, packed[first:last], needed, slots, first, bands, ties)

    def over_core(sent):
        return send(sent, "lon", lambda s: s ^ 1)

    def added(kept, core):
        return (kept + core.astype(jnp.float32)).astype(jnp.bfloat16)

    def over_y(value):
        return send(value, "lon", lambda s: s ^ 2)

    every = tuple(range(MAXS))
    sums = []
    conv0 = convolved(0, every, [])
    kept_a, sent_a = mix(conv0, every, [ours], longitudes, [planes[0][1][1], planes[2][1][1]])
    core_a = over_core(sent_a)
    part_a = added(kept_a[1], core_a[1])
    across_a = over_y(part_a)
    early = gelu_of(kept_a, core_a, across_a)
    kept_b, sent_b = mix(conv0, every, [theirs], longitudes, [])
    core_b = over_core(sent_b)
    part_b = added(kept_b[1], core_b[1])
    across_b = over_y(part_b)
    sums.append((cuts[0][0], (1,), kept_b, core_b, across_b))
    conv1 = convolved(1, every, [])
    kept, sent = mix(conv1, every, [ours, theirs], longitudes, [across_a])
    core = over_core(sent)
    sums.append((cuts[1][0], (0, 1), kept, core, over_y(added(kept[1], core[1]))))
    return finish(turned.reshape(1).astype(jnp.int32), early, sums, ours.shape[1], bands)


def solution(mesh):
    placed = (P("groups", "lon", None), P("groups"), P(None, "groups", None, None), P("lon", None))
    return jax.shard_map(
        on_device, mesh=mesh, in_specs=placed, out_specs=P("groups", "lon", None), check_vma=False
    )
```

```python
import jax
import jax.numpy as jnp
from jax import lax
from jax.experimental import pallas as pl
from jax.experimental.pallas import tpu as pltpu
from jax.sharding import PartitionSpec as P

MAXS = 4
UNIT = 16
VMEM = 28 << 20
WORK = 9_000_000_000


def send(value, axis, target_of):
    count = lax.axis_size(axis)
    return lax.ppermute(value, axis, [(s, target_of(s)) for s in range(count)])


def round_up(value, step):
    return -(-value // step) * step


def lay_out(pieces, first, last, ties):
    shape = (len(pieces), last - first, *pieces[0].shape[1:])

    def body(*refs):
        for n in range(len(pieces)):
            refs[-1][n] = refs[n][first:last]

    return pl.pallas_call(
        body,
        in_specs=[pl.BlockSpec(memory_space=pltpu.VMEM)] * len(pieces)
        + [pl.BlockSpec(memory_space=pl.ANY)] * len(ties),
        out_specs=pl.BlockSpec(memory_space=pltpu.VMEM),
        out_shape=jax.ShapeDtypeStruct(shape, pieces[0].dtype),
        compiler_params=pltpu.CompilerParams(vmem_limit_bytes=VMEM),
        name="lay_out",
    )(*pieces, *ties)


def packed_basis(basis_table, support, longitudes, segment):
    filters, bands, three, offsets = basis_table.shape
    distance = jnp.abs(jnp.arange(offsets) - MAXS * longitudes)
    within = distance[None, :] <= (support * longitudes)[:, None]
    rows = jnp.where(within[None, :, None, :], basis_table, jnp.zeros_like(basis_table))
    rows = jnp.pad(rows, ((0, 0), (0, 0), (0, 0), (0, segment - offsets)))
    rows = rows.transpose(1, 0, 2, 3).reshape(bands, filters, three * segment)
    return rows.astype(jnp.float32)


def fill_toeplitz(row_of, out_ref, filters, longitudes):
    rows, lanes = out_ref.shape

    def block(k):
        row = jnp.broadcast_to(row_of(k), (longitudes, lanes))
        return pltpu.roll(row, 0, 1, stride=1, stride_axis=0)

    for k in range(0, filters, 2):
        start = k * longitudes
        if k + 1 < filters:
            pair = jnp.concatenate([block(k), block(k + 1)], 0)
        else:
            tail = jnp.zeros((rows - start - longitudes, lanes), jnp.float32)
            pair = jnp.concatenate([block(k), tail], 0)
        out_ref[start : start + pair.shape[0], :] = pair.astype(jnp.bfloat16)


def convolve(place, packed, planes, slots, first, bands, ties):
    longitudes, chans = planes[0][0][1].shape[2:]
    count, filters, lanes = packed.shape
    rows = round_up(filters * longitudes, UNIT)
    segment = lanes // 3
    span = 3 * MAXS * longitudes
    low, high = max(first - 1, 0), min(first + count + 1, bands)
    arrays, found = [], [{}, {}, {}]
    for t in range(3):
        for start, array in planes[t]:
            for b in range(array.shape[1]):
                found[t][start + b] = (len(arrays), b)
            arrays.append(array)

    def body(place_ref, packed_ref, *refs):
        ins, (mixin, line, windows, toeplitz) = refs[: len(arrays)], refs[len(arrays) + len(ties) :]
        here = place_ref[0]
        line[:, span:, :] = jnp.zeros((2, line.shape[1] - span, chans), jnp.float32)
        for b in range(low, high):
            side = b % 2
            for t in range(3):
                which, at = found[t][b]
                for p in range(MAXS):
                    start = (t * MAXS + p) * longitudes
                    line[side, start : start + longitudes, :] = ins[which][p ^ here, at].astype(jnp.float32)
            start = (b - low) * segment
            for n, r in enumerate(slots):
                begin = pl.multiple_of((r ^ here) * longitudes, 8)
                part = line[side, pl.ds(begin, segment), :].astype(jnp.bfloat16)
                windows[start : start + segment, n * chans : (n + 1) * chans] = part
        for c in range(count):
            i = first + c
            from_band, to_band = max(i - 1, 0), min(i + 2, bands)
            matrix = toeplitz.at[c % 2]
            fill_toeplitz(lambda k, c=c: packed_ref[c, k : k + 1, :], matrix, filters, longitudes)
            matrix = matrix[:, (from_band - i + 1) * segment : (to_band - i + 1) * segment]
            window = windows[(from_band - low) * segment : (to_band - low) * segment, :]
            conv = jnp.dot(matrix, window, preferred_element_type=jnp.float32)
            for pair in range(0, len(slots), 2):
                rows_of = []
                for n in (pair, pair + 1):
                    parts = [
                        conv[k * longitudes : (k + 1) * longitudes, n * chans : (n + 1) * chans]
                        for k in range(filters)
                    ]
                    rows_of.append(jnp.concatenate(parts, 1))
                start = (pair // 2 * count + c) * 2 * longitudes
                mixin[start : start + 2 * longitudes, :] = jnp.concatenate(rows_of, 0).astype(jnp.bfloat16)

    vmem = pl.BlockSpec(memory_space=pltpu.VMEM)
    return pl.pallas_call(
        body,
        in_specs=[pl.BlockSpec(memory_space=pltpu.SMEM)]
        + [vmem] * (1 + len(arrays))
        + [pl.BlockSpec(memory_space=pl.ANY)] * len(ties),
        out_specs=vmem,
        out_shape=jax.ShapeDtypeStruct((count * len(slots) * longitudes, filters * chans), jnp.bfloat16),
        scratch_shapes=[
            pltpu.VMEM((2, round_up((MAXS - 1) * longitudes + max(segment, span), 8), chans), jnp.float32),
            pltpu.VMEM(((high - low) * segment, len(slots) * chans), jnp.bfloat16),
            pltpu.VMEM((2, rows, lanes), jnp.bfloat16),
        ],
        compiler_params=pltpu.CompilerParams(vmem_limit_bytes=VMEM),
        cost_estimate=pl.CostEstimate(
            flops=WORK, bytes_accessed=1, transcendentals=0
        ),
        name="convolve",
    )(place, packed, *arrays, *ties)


def mix(convolved, slots, weights, longitudes, ties):
    pair = convolved.shape[0] // (MAXS // 2)
    count = pair // (2 * longitudes)
    half = len(slots) // 2
    width = weights[0].shape[1]
    begin = slots[0] // 2 * pair

    def body(conv_ref, *refs):
        kept_ref, sent_ref = refs[-2:]
        block = conv_ref[begin : begin + half * pair, :]
        for n in range(len(weights)):
            mixed = jnp.dot(block, refs[n][...], preferred_element_type=jnp.float32)
            for h in range(half):
                for c in range(count):
                    start = h * pair + c * 2 * longitudes
                    value = mixed[start : start + longitudes]
                    kept_ref[h, c, :, n * width : (n + 1) * width] = value
                    value = mixed[start + longitudes : start + 2 * longitudes].astype(jnp.bfloat16)
                    sent_ref[h, c, :, n * width : (n + 1) * width] = value

    vmem = pl.BlockSpec(memory_space=pltpu.VMEM)
    shape = (half, count, longitudes, len(weights) * width)
    return pl.pallas_call(
        body,
        in_specs=[vmem] * (1 + len(weights)) + [pl.BlockSpec(memory_space=pl.ANY)] * len(ties),
        out_specs=[vmem, vmem],
        out_shape=[jax.ShapeDtypeStruct(shape, jnp.float32), jax.ShapeDtypeStruct(shape, jnp.bfloat16)],
        compiler_params=pltpu.CompilerParams(vmem_limit_bytes=VMEM),
        name="mix",
    )(convolved, *weights, *ties)


def gelu_of(kept, core, across):
    def body(kept_ref, core_ref, across_ref, out_ref):
        total = kept_ref[0] + core_ref[0].astype(jnp.float32) + across_ref[...].astype(jnp.float32)
        out_ref[...] = jax.nn.gelu(total).astype(jnp.bfloat16)

    vmem = pl.BlockSpec(memory_space=pltpu.VMEM)
    return pl.pallas_call(
        body,
        in_specs=[vmem] * 3,
        out_specs=vmem,
        out_shape=jax.ShapeDtypeStruct(across.shape, jnp.bfloat16),
        compiler_params=pltpu.CompilerParams(vmem_limit_bytes=VMEM),
        name="gelu_of",
    )(kept, core, across)


def finish(turned, early, sums, width, bands):
    longitudes = sums[0][2].shape[2]
    ready = early[0].shape[0]

    def body(turned_ref, *refs):
        early_refs, refs = refs[: len(early)], refs[len(early) :]
        out_ref, held, sems = refs[-3:]
        for band in range(bands):
            if band < ready:
                for half, early_ref in enumerate(early_refs):
                    column = pl.multiple_of((turned_ref[0] ^ half) * width, width)
                    held[band, :, pl.ds(column, width)] = early_ref[band]
            for n, (first, halves, kept, _, _) in enumerate(sums):
                at = band - first
                if not 0 <= at < kept.shape[1]:
                    continue
                kept_ref, core_ref, across_ref = refs[3 * n : 3 * n + 3]
                for m, half in enumerate(halves):
                    column = pl.multiple_of((turned_ref[0] ^ half) * width, width)
                    from_ = slice(m * width, (m + 1) * width)
                    total = kept_ref[0, at, :, from_] + core_ref[0, at, :, from_].astype(jnp.float32)
                    total += across_ref[at, :, from_].astype(jnp.float32)
                    held[band, :, pl.ds(column, width)] = jax.nn.gelu(total).astype(jnp.bfloat16)
            pltpu.make_async_copy(held.at[band], out_ref.at[band], sems.at[band]).start()
        for band in range(bands):
            pltpu.make_async_copy(held.at[band], out_ref.at[band], sems.at[band]).wait()

    vmem = pl.BlockSpec(memory_space=pltpu.VMEM)
    return pl.pallas_call(
        body,
        in_specs=[pl.BlockSpec(memory_space=pltpu.SMEM)] + [vmem] * (len(early) + 3 * len(sums)),
        out_specs=pl.BlockSpec(memory_space=pl.ANY),
        out_shape=jax.ShapeDtypeStruct((bands, longitudes, 2 * width), jnp.bfloat16),
        scratch_shapes=[
            pltpu.VMEM((bands, longitudes, 2 * width), jnp.bfloat16),
            pltpu.SemaphoreType.DMA((bands,)),
        ],
        compiler_params=pltpu.CompilerParams(vmem_limit_bytes=VMEM),
        name="finish",
    )(turned, *early, *(array for entry in sums for array in entry[2:]))


def gather_weights(mixing, filters, channels):
    held, outs = mixing.shape
    chans = channels // MAXS
    width = outs // 2
    devices = lax.axis_size("lon")
    groups = lax.axis_size("groups")
    lon = lax.axis_index("lon")
    place = lon % MAXS
    planes = devices // MAXS
    units = held // UNIT
    per_filter = channels // UNIT
    per_quarter = chans // UNIT
    fits = (
        groups == 2
        and planes == MAXS
        and held % UNIT == 0
        and (MAXS * units) % per_filter == per_quarter
    )
    if not fits:
        whole = lax.all_gather(mixing, "lon", axis=0, tiled=True).reshape(filters, channels, outs)
        mine = lax.dynamic_slice_in_dim(whole, place * chans, chans, 1).reshape(filters * chans, outs)
        return (), lambda *_: (mine[:, :width], mine[:, width:], jnp.int32(0))
    group = lax.axis_index("groups")
    plane = lon // MAXS
    rows = lax.dynamic_slice_in_dim(mixing, group * width, width, 1)
    far = send(rows, "lon", lambda s: s ^ (2 * MAXS))
    near = send(rows, "lon", lambda s: s ^ MAXS)
    rows = jnp.stack([rows, near, far, send(far, "lon", lambda s: s ^ MAXS)])
    rows = rows.reshape(planes, units, UNIT, width)
    base = (place * units + jnp.arange(units)) % per_filter // per_quarter

    def for_quarter(quarter):
        entry = ((quarter - base) % MAXS) ^ plane
        picked = rows[0]
        for z in range(1, planes):
            picked = jnp.where((entry == z)[:, None, None], rows[z], picked)
        return picked

    pieces = {0: for_quarter(place)}
    for r in (3, 2, 1):
        pieces[r] = send(for_quarter(place ^ r), "lon", lambda s, r=r: s ^ r)
    def sort(*ties):
        mine = jnp.concatenate([pieces[r] for r in range(MAXS)])
        count = filters * per_quarter
        wanted = jnp.arange(count)
        source = wanted // per_quarter * per_filter + place * per_quarter + wanted % per_quarter
        position = (source // units % MAXS ^ place) * units + source % units

        def body(position_ref, mine_ref, *refs):
            for u in range(count):
                refs[-1][u * UNIT : (u + 1) * UNIT, :] = mine_ref[position_ref[u]]

        ours = pl.pallas_call(
            body,
            in_specs=[pl.BlockSpec(memory_space=pltpu.SMEM), pl.BlockSpec(memory_space=pltpu.VMEM)]
            + [pl.BlockSpec(memory_space=pl.ANY)] * len(ties),
            out_specs=pl.BlockSpec(memory_space=pltpu.VMEM),
            out_shape=jax.ShapeDtypeStruct((filters * chans, width), mixing.dtype),
            compiler_params=pltpu.CompilerParams(vmem_limit_bytes=VMEM),
            name="sort_weights",
        )(position.astype(jnp.int32), mine, *ties)
        return ours, send(ours, "groups", lambda s: s ^ 1), group

    return (pieces[1], pieces[2], pieces[3]), sort


def on_device(inputs, support, basis_table, mixing):
    bands, longitudes, channels = inputs.shape
    filters = basis_table.shape[0]
    chans = channels // MAXS
    devices = lax.axis_size("lon")
    place = lax.axis_index("lon") % MAXS
    segment = round_up((2 * MAXS + 1) * longitudes, 128)
    packed = packed_basis(basis_table, support, longitudes, segment)
    cuts = ((0, 6), (6, 8))

    def quarter(r):
        return lax.dynamic_slice_in_dim(inputs, (place ^ r) * chans, chans, 2)

    pieces = {0: quarter(0)}
    for r in (3, 2, 1):
        pieces[r] = send(quarter(r), "lon", lambda s, r=r: s ^ r)
    arrived, sort = gather_weights(mixing, filters, channels)
    planes = [[], [], []]
    reached = 0
    for index, (first, last) in enumerate(cuts):
        until = min(last + 1, bands)
        ties = list(arrived) if index else []
        own = lay_out([pieces[r] for r in range(MAXS)], reached, until, ties)
        west = send(own, "lon", lambda s: (s + MAXS) % devices)
        east = send(own, "lon", lambda s: (s - MAXS) % devices)
        for held, array in zip(planes, (west, own, east)):
            held.append((reached, array))
        reached = until
    ours, theirs, turned = sort()

    here = place.reshape(1).astype(jnp.int32)

    def convolved(index, slots, ties):
        first, last = cuts[index]
        low, high = max(first - 1, 0), min(last + 1, bands)
        needed = [[(s, a) for s, a in held if s < high and s + a.shape[1] > low] for held in planes]
        return convolve(here, packed[first:last], needed, slots, first, bands, ties)

    def over_core(sent):
        return send(sent, "lon", lambda s: s ^ 1)

    def added(kept, core):
        return (kept + core.astype(jnp.float32)).astype(jnp.bfloat16)

    def over_y(value):
        return send(value, "lon", lambda s: s ^ 2)

    every = tuple(range(MAXS))
    sums = []
    conv0 = convolved(0, every, [])
    kept_a, sent_a = mix(conv0, every, [ours], longitudes, [planes[0][1][1], planes[2][1][1]])
    core_a = over_core(sent_a)
    part_a = added(kept_a[1], core_a[1])
    across_a = over_y(part_a)
    early = [gelu_of(kept_a, core_a, across_a)]
    kept_b, sent_b = mix(conv0, every, [theirs], longitudes, [])
    core_b = over_core(sent_b)
    part_b = added(kept_b[1], core_b[1])
    across_b = over_y(part_b)
    early.append(gelu_of(kept_b, core_b, across_b))
    conv1 = convolved(1, every, [])
    kept, sent = mix(conv1, every, [ours, theirs], longitudes, [across_a])
    core = over_core(sent)
    sums.append((cuts[1][0], (0, 1), kept, core, over_y(added(kept[1], core[1]))))
    return finish(turned.reshape(1).astype(jnp.int32), early, sums, ours.shape[1], bands)


def solution(mesh):
    placed = (P("groups", "lon", None), P("groups"), P(None, "groups", None, None), P("lon", None))
    return jax.shard_map(
        on_device, mesh=mesh, in_specs=placed, out_specs=P("groups", "lon", None), check_vma=False
    )
```
